1024 devices in a mesh: fsdp: 128 (over y, z, core), rep: 8 (over x).
Axes of the slice: x: 8, y: 8, z: 8, core: 2. Of those that a mesh axis runs over, the one named last changes fastest.
Arguments:
- acts: bfloat16 [8, 65536, 128], P('rep', 'fsdp'), may hold values from -6 to 6
- cotan: bfloat16 [8, 65536, 2560], P('rep', 'fsdp'), may hold values from -6 to 6
- weight: bfloat16 [128, 2560], P('fsdp'), may hold values from -0.5 to 0.5
- momentum: float32 [8, 128, 2560], P('rep', 'fsdp'), may hold values from -6 to 6
- select_ids: int32 [8, 128, 40, 8], P('rep', 'fsdp'), may hold values from 0 to 63, as said below
Outputs:
- new_momentum: float32 [8, 128, 2560], P('rep', 'fsdp')
- dacts: bfloat16 [8, 65536, 128], P('rep', 'fsdp')
- update: float32 [128, 2560], P('fsdp')
The draws below stay inside these ranges and needn't reach their ends.
Inputs may be any that keep to these rules, and one draw needn't show every extreme that they name: `select_ids`: the 8 positions of each segment are distinct.
All inputs are finite; a program needn't handle non-finite values.
Results may differ from the reference program's by a relative error of at most 0.0049.
Values may be sent and summed in bfloat16 or wider, within the bound.
No kernel may reach another device: no remote copies, remote signals or barrier semaphores. Data moves between devices by JAX's collectives and lax.ppermute only.
A program may use at most 32 MiB of HBM per device.

```python
import math
import jax
import jax.numpy as jnp
from jax import lax

D = 2560
KWIN = 128
TOK_DEV = 512
SPAN = 64
TOPC = 8
TOKENS = 65536
N_FSDP = 128
N_REP = 8


def draw_select_ids(key, part):
    key = jax.random.fold_in(key, 7)
    scores = jax.random.randint(key, (N_REP, KWIN, D // SPAN, SPAN), 0, 1 << 20)
    scores = scores * SPAN + jnp.arange(SPAN).astype(jnp.int32)
    order = jnp.argsort(scores, axis=-1)[..., :TOPC]
    return order.astype(jnp.int32)


def shard_levels(rng, extent, cuts, smallest, high):
    gain = 1.0
    for position, parts in cuts:
        heights = jax.random.uniform(jax.random.fold_in(jax.random.fold_in(rng, 6), position), (parts,), jnp.float32, smallest / len(cuts), high / len(cuts))
        gain = gain * jnp.repeat(jnp.exp(heights), extent[position] // parts).reshape((-1,) + (1,) * (len(extent) - 1 - position))
    return gain


def scatter_about(rng, extent, scale, most, split=(), held_as=jnp.bfloat16):
    array = scale * jax.random.normal(rng, extent, jnp.float32)
    if split:
        array = array * shard_levels(rng, extent, split, -0.22, 0.18)
    return jnp.clip(array, -most, most).astype(held_as)


def setup_inputs(seed: int = 0) -> dict:
    keys = jax.random.split(jax.random.key(seed), 6)
    return {
        "acts": scatter_about(keys[0], (N_REP, TOKENS, KWIN), 1.0, 6.0, ((0, 8), (1, 128))),
        "cotan": scatter_about(keys[1], (N_REP, TOKENS, D), 1.0, 6.0, ((0, 8), (1, 128))),
        "weight": scatter_about(keys[2], (KWIN, D), KWIN ** -0.5, 0.5, ((0, 128),)),
        "momentum": scatter_about(keys[3], (N_REP, KWIN, D), 1.0, 6.0, ((0, 8), (1, 128)), jnp.float32),
        "select_ids": draw_select_ids(jax.random.fold_in(keys[5], 71), 0),
    }


def dct_table():
    index = jnp.arange(SPAN).astype(jnp.float32)
    freq = index[:, None]
    factor = jnp.where(freq == 0.0, jnp.sqrt(1.0 / SPAN), jnp.sqrt(2.0 / SPAN))
    return factor * jnp.cos(jnp.pi * (index[None, :] + 0.5) * freq / SPAN)

def make_group(weight):

    def one_group(items):
        acts_r, cotan_r, moment_r, ids_r = items
        table = dct_table()
        scale = 1.0 / math.sqrt(N_FSDP * TOK_DEV)
        pre = jnp.dot(acts_r, weight, preferred_element_type=jnp.float32)
        sig = jax.nn.sigmoid(pre)
        dpre = (cotan_r.astype(jnp.float32) * sig * (1.0 + pre * (1.0 - sig))).astype(jnp.bfloat16)
        dacts = jnp.dot(dpre, weight.T, preferred_element_type=jnp.float32).astype(jnp.bfloat16)
        grad = jnp.dot(acts_r.T, dpre, preferred_element_type=jnp.float32) * scale
        moment = 0.9 * moment_r + grad
        blocks = moment.reshape(KWIN, D // SPAN, SPAN)
        coeffs = jnp.einsum('rcn,kn->rck', blocks, table, precision=lax.Precision.HIGHEST)
        onehot = (ids_r[..., None] == jnp.arange(SPAN).astype(jnp.int32)).astype(jnp.float32)
        kept = jnp.einsum('rck,rcjk->rcj', coeffs, onehot, precision=lax.Precision.HIGHEST)
        dense = jnp.einsum('rcj,rcjk->rck', kept, onehot, precision=lax.Precision.HIGHEST)
        decoded = jnp.einsum('rck,kn->rcn', dense, table, precision=lax.Precision.HIGHEST).reshape(KWIN, D)
        return (moment - decoded, dacts, decoded)
    return one_group

def reference(acts, cotan, weight, momentum, select_ids):
    new_momentum, dacts, decoded = lax.map(make_group(weight), (acts, cotan, momentum, select_ids))
    update = lax.optimization_barrier(jnp.sum(decoded, axis=0)) / N_REP
    return (new_momentum, dacts, update)
```

```python
import math

import jax
import jax.numpy as jnp
from jax import lax
from jax.sharding import Mesh
from jax.sharding import PartitionSpec as P

ROWS = ("y", "z", "core")
CHIPS = ("y", "z")


def dct_table(length):
    index = jnp.arange(length).astype(jnp.float32)
    freq = index[:, None]
    factor = jnp.where(freq == 0.0, jnp.sqrt(1.0 / length), jnp.sqrt(2.0 / length))
    return factor * jnp.cos(jnp.pi * (index[None, :] + 0.5) * freq / length)


def local(acts, cotan, weight, momentum, select_ids):
    upstream = cotan[0]
    tok_rows, depth = acts.shape[1:]
    width = momentum.shape[2]
    segments = select_ids.shape[2]
    length = width // segments
    groups = lax.axis_size("rep")
    chips = lax.axis_size(CHIPS)
    cores = lax.axis_size("core")
    core = lax.axis_index("core")
    scale = 1.0 / math.sqrt(lax.axis_size(ROWS) * tok_rows)
    inputs = acts[0].reshape(tok_rows, chips, cores).transpose(0, 2, 1).reshape(tok_rows, depth)
    sent = jnp.broadcast_to(weight[None], (chips, 1, width))
    rows = lax.all_to_all(sent, CHIPS, 0, 0, tiled=True).reshape(chips, width)
    whole = lax.all_gather(rows, "core", axis=0, tiled=True)
    pre = jnp.dot(inputs, whole, preferred_element_type=jnp.float32)
    sig = jax.nn.sigmoid(pre)
    dpre = (upstream.astype(jnp.float32) * sig * (1.0 + pre * (1.0 - sig))).astype(jnp.bfloat16)
    contract = (((0,), (0,)), ((), ()))
    term = lax.dot_general(inputs, dpre, contract, preferred_element_type=jnp.float32) * scale
    term = term.reshape(cores, chips, width)
    mine = lax.dynamic_index_in_dim(term, core, 0, keepdims=False)
    other = lax.dynamic_index_in_dim(term, 1 - core, 0, keepdims=False).astype(jnp.bfloat16)
    both = lax.all_gather(other, "core", axis=0, tiled=False)
    got = lax.dynamic_index_in_dim(both, 1 - core, 0, keepdims=False)
    chip_sum = (mine + got.astype(jnp.float32)).astype(jnp.bfloat16)
    parts = lax.all_to_all(chip_sum[:, None, :], CHIPS, 0, 0, tiled=True)
    grad = jnp.sum(parts.astype(jnp.float32), axis=0)
    backward = (((1,), (1,)), ((), ()))
    input_grad = lax.dot_general(dpre, whole, backward, preferred_element_type=jnp.float32)
    dacts = input_grad.astype(jnp.bfloat16)
    dacts = dacts.reshape(tok_rows, cores, chips).transpose(0, 2, 1).reshape(1, tok_rows, depth)
    table = dct_table(length)
    moment = 0.9 * momentum[0] + grad
    blocks = moment.reshape(segments, length)
    coeffs = jnp.einsum("cn,kn->ck", blocks, table, precision=lax.Precision.HIGHEST)
    positions = jnp.arange(length)
    chosen = jnp.any(select_ids[0, 0][..., None] == positions, axis=1)
    dense = jnp.where(chosen, coeffs, 0.0)
    decoded = jnp.einsum("ck,kn->cn", dense, table, precision=lax.Precision.HIGHEST).reshape(1, width)
    new_momentum = (moment - decoded)[None]
    spread = jnp.broadcast_to(decoded[None], (groups, 1, width))
    decoded_all = lax.all_to_all(spread, "rep", 0, 0, tiled=True)
    update = jnp.sum(decoded_all, axis=0) / groups
    return (new_momentum, dacts, update)


def solution(mesh):
    shape = (8, 8, 2, mesh.shape["rep"])
    split = Mesh(mesh.devices.reshape(shape), (*ROWS, "rep"))
    placed = (
        P("rep", ROWS, None),
        P("rep", ROWS, None),
        P(ROWS, None),
        P("rep", ROWS, None),
        P("rep", ROWS, None, None),
    )
    return jax.shard_map(
        local,
        mesh=split,
        in_specs=placed,
        out_specs=(P("rep", ROWS, None), P("rep", ROWS, None), P(ROWS, None)),
        check_vma=False,
    )
```

```python
import math

import jax
import jax.numpy as jnp
from jax import lax
from jax.experimental import pallas as pl
from jax.experimental.pallas import tpu as pltpu
from jax.sharding import Mesh
from jax.sharding import PartitionSpec as P

ROWS = ("y", "z", "core")
CHIPS = ("y", "z")
LANES = 128
CHUNK = 256
HIGHEST = lax.Precision.HIGHEST
F32 = jnp.float32
BF16 = jnp.bfloat16
VMEM = pl.BlockSpec(memory_space=pltpu.VMEM)
SMEM = pl.BlockSpec(memory_space=pltpu.SMEM)


def params():
    return pltpu.CompilerParams(vmem_limit_bytes=40 * 1024 * 1024)


def dct_table(length):
    index = jnp.arange(length).astype(F32)
    freq = index[:, None]
    factor = jnp.where(freq == 0.0, jnp.sqrt(1.0 / length), jnp.sqrt(2.0 / length))
    return factor * jnp.cos(jnp.pi * (index[None, :] + 0.5) * freq / length)


def backward_kernel(scale, core_ref, acts_ref, cotan_ref, whole_ref, mine_ref, other_ref, dpre_ref):
    cores, chips, width = whole_ref.shape
    depth = cores * chips
    acts = acts_ref[...]
    out = lax.broadcasted_iota(jnp.int32, (depth, depth), 0)
    col = lax.broadcasted_iota(jnp.int32, (depth, depth), 1)
    order = jnp.where(out < chips, out * 2, (out - chips) * 2 + 1)
    place = (order == col).astype(BF16)
    turned = (((1,), (1,)), ((), ()))
    acts_t = lax.dot_general(place, acts, turned, preferred_element_type=F32).astype(BF16)
    half = (lax.dot_general(acts, place, turned, preferred_element_type=F32) * 0.5).astype(BF16)
    first = core_ref[0] == 0
    for lo in range(0, width, CHUNK):
        part = pl.ds(lo, CHUNK)
        slab = whole_ref[:, :, part].reshape(depth, CHUNK)
        mid = jnp.dot(half, slab, preferred_element_type=F32)
        t = jnp.tanh(mid)
        slope = (1.0 + t) * (1.0 + mid * (1.0 - t))
        dpre = (cotan_ref[:, part].astype(F32) * slope).astype(BF16)
        dpre_ref[:, part] = dpre
        term = jnp.dot(acts_t, dpre, preferred_element_type=F32) * scale
        top, low = term[:chips], term[chips:]
        mine_ref[:, part] = jnp.where(first, top, low)
        other_ref[:, part] = jnp.where(first, low, top).astype(BF16)


def pair_kernel(core_ref, mine_ref, both_ref, out_ref):
    chips, width = mine_ref.shape
    got = both_ref[1 - core_ref[0]].astype(F32)
    total = (mine_ref[...] + got).astype(BF16)
    out_ref[...] = jnp.stack([total[:, : width // 2], total[:, width // 2 :]], axis=1)


def select_kernel(parts_ref, carried_ref, mask_ref, table_ref, spread_ref, kept_ref):
    chips, halves, span = parts_ref.shape
    tiles = span // LANES
    grad = jnp.sum(parts_ref[...].astype(F32), axis=0)
    grad = jnp.concatenate([grad[:, q * LANES : (q + 1) * LANES] for q in range(tiles)], axis=0)
    moment = carried_ref[...] + grad
    table = table_ref[...]
    turned = (((1,), (1,)), ((), ()))
    coeffs = lax.dot_general(moment, table, turned, precision=HIGHEST, preferred_element_type=F32)
    dense = jnp.where(mask_ref[...] != 0.0, coeffs, 0.0)
    decoded = jnp.dot(dense, table, precision=HIGHEST, preferred_element_type=F32)
    spread_ref[...] = jnp.broadcast_to(decoded[None], spread_ref.shape)
    kept_ref[...] = moment - decoded


def row_order(tiles, width):
    count = tiles.shape[0] // 2
    return tiles.reshape(count, 2, LANES).transpose(1, 0, 2).reshape(1, width)


def local(acts, cotan, weight, momentum, select_ids):
    tok_rows, depth = acts.shape[1:]
    width = momentum.shape[2]
    segments = select_ids.shape[2]
    length = width // segments
    groups = lax.axis_size("rep")
    chips = lax.axis_size(CHIPS)
    cores = lax.axis_size("core")
    core = lax.axis_index("core").reshape(1).astype(jnp.int32)
    scale = 1.0 / math.sqrt(lax.axis_size(ROWS) * tok_rows)
    span = width // 2
    tiles = span // LANES
    sent = jnp.broadcast_to(weight.reshape(1, 2, span), (chips, 2, span))
    rows = lax.all_to_all(sent, CHIPS, 0, 0, tiled=True).reshape(chips, width)
    whole = lax.all_gather(rows, "core", axis=0, tiled=False)
    mine, other, dpre = pl.pallas_call(
        lambda *refs: backward_kernel(scale * 0.5, *refs),
        out_shape=(
            jax.ShapeDtypeStruct((chips, width), F32),
            jax.ShapeDtypeStruct((chips, width), BF16),
            jax.ShapeDtypeStruct((tok_rows, width), BF16),
        ),
        in_specs=[SMEM, VMEM, VMEM, VMEM],
        out_specs=(VMEM, VMEM, VMEM),
        compiler_params=params(),
        cost_estimate=pl.CostEstimate(
            flops=4 * tok_rows * depth * width, bytes_accessed=4 * tok_rows * width, transcendentals=tok_rows * width
        ),
        name="backward",
    )(core, acts[0], cotan[0], whole)
    both = lax.all_gather(other, "core", axis=0, tiled=False)
    chip_sum = pl.pallas_call(
        pair_kernel,
        out_shape=jax.ShapeDtypeStruct((chips, 2, span), BF16),
        in_specs=[SMEM, VMEM, VMEM],
        out_specs=VMEM,
        compiler_params=params(),
        name="pair",
    )(core, mine, both)
    parts = lax.all_to_all(chip_sum, CHIPS, 0, 0, tiled=True)
    turned = (((1,), (1,)), ((), ()))
    input_grad = lax.dot_general(
        dpre, whole.reshape(depth, width), turned, preferred_element_type=F32
    )
    dacts = (input_grad * 0.5).astype(BF16)
    dacts = dacts.reshape(tok_rows, cores, chips).transpose(0, 2, 1).reshape(1, tok_rows, depth)
    table = jnp.kron(jnp.eye(LANES // length, dtype=F32), dct_table(length))
    carried = (0.9 * momentum).reshape(2, tiles, LANES).transpose(1, 0, 2).reshape(2 * tiles, LANES)
    ids = select_ids.reshape(2, tiles, LANES // length, -1).transpose(1, 0, 2, 3)
    mask = jnp.any(ids[..., None] == jnp.arange(length), axis=3)
    mask = mask.reshape(2 * tiles, LANES).astype(F32)
    spread, kept = pl.pallas_call(
        select_kernel,
        out_shape=(
            jax.ShapeDtypeStruct((groups, 2 * tiles, LANES), F32),
            jax.ShapeDtypeStruct((2 * tiles, LANES), F32),
        ),
        in_specs=[VMEM] * 4,
        out_specs=(VMEM, VMEM),
        compiler_params=params(),
        name="select",
    )(parts, carried, mask, table)
    new_momentum = row_order(kept, width)[None]
    decoded_all = lax.all_to_all(spread, "rep", 0, 0, tiled=True)
    update = row_order(jnp.sum(decoded_all, axis=0) / groups, width)
    return (new_momentum, dacts, update)


def solution(mesh):
    shape = (8, 8, 2, mesh.shape["rep"])
    split = Mesh(mesh.devices.reshape(shape), (*ROWS, "rep"))
    placed = (
        P("rep", ROWS, None),
        P("rep", ROWS, None),
        P(ROWS, None),
        P("rep", ROWS, None),
        P("rep", ROWS, None, None),
    )
    return jax.shard_map(
        local,
        mesh=split,
        in_specs=placed,
        out_specs=(P("rep", ROWS, None), P("rep", ROWS, None), P(ROWS, None)),
        check_vma=False,
    )
```

```python
import math

import jax
import jax.numpy as jnp
from jax import lax
from jax.experimental import pallas as pl
from jax.experimental.pallas import tpu as pltpu
from jax.sharding import Mesh
from jax.sharding import PartitionSpec as P

ROWS = ("y", "z", "core")
CHIPS = ("y", "z")
PEERS = ("rep", "core")
LANES = 128
HIGHEST = lax.Precision.HIGHEST
TURNED = (((1,), (1,)), ((), ()))
F32 = jnp.float32
BF16 = jnp.bfloat16
VMEM = pl.BlockSpec(memory_space=pltpu.VMEM)
ANY = pl.BlockSpec(memory_space=pl.ANY)
SMEM = pl.BlockSpec(memory_space=pltpu.SMEM)


def params(mib):
    return pltpu.CompilerParams(vmem_limit_bytes=mib * 1024 * 1024)


def dct_table(length):
    index = jnp.arange(length).astype(F32)
    freq = index[:, None]
    factor = jnp.where(freq == 0.0, jnp.sqrt(1.0 / length), jnp.sqrt(2.0 / length))
    return factor * jnp.cos(jnp.pi * (index[None, :] + 0.5) * freq / length)


def backward_kernel(scale, acts_hbm, cotan_hbm, whole_hbm, term_ref, dacts_ref, acts_ref, cotan_ref, whole_ref, sems):
    cores, chips, halves, span = whole_hbm.shape
    depth = cores * chips
    weight = pltpu.make_async_copy(whole_hbm, whole_ref, sems.at[halves + 1])
    weight.start()
    copies = [pltpu.make_async_copy(acts_hbm, acts_ref, sems.at[halves])]
    for half in range(halves):
        part = pl.ds(half * span, span)
        copies.append(pltpu.make_async_copy(cotan_hbm.at[:, part], cotan_ref.at[half], sems.at[half]))
    for copy in copies:
        copy.start()
    weight.wait()
    held = whole_ref[...].reshape(depth * halves, span)
    row = lax.broadcasted_iota(jnp.int32, (depth, depth * halves), 0)
    col = lax.broadcasted_iota(jnp.int32, (depth, depth * halves), 1)
    slabs = []
    for half in range(halves):
        source = ((row % cores) * chips + row // cores) * halves + half
        place = (source == col).astype(BF16)
        slabs.append(jnp.dot(place, held, preferred_element_type=F32).astype(BF16))
    copies[0].wait()
    acts = acts_ref[...]
    halved = (acts.astype(F32) * 0.5).astype(BF16)
    acts_t = acts.T
    total = None
    for half, slab in enumerate(slabs):
        mid = jnp.dot(halved, slab, preferred_element_type=F32)
        t = jnp.tanh(mid)
        slope = (1.0 + t) * (1.0 + mid * (1.0 - t))
        copies[half + 1].wait()
        part = slice(half * span, (half + 1) * span)
        dpre = (cotan_ref[half].astype(F32) * slope).astype(BF16)
        term = jnp.dot(acts_t, dpre, preferred_element_type=F32) * scale
        term_ref[:, :, part] = term.astype(BF16).reshape(chips, cores, span)
        back = lax.dot_general(dpre, slab, TURNED, preferred_element_type=F32)
        total = back if total is None else total + back
    dacts_ref[...] = (total * 0.5).astype(BF16)


def select_kernel(parts_ref, carried_ref, mask_ref, table_ref, spread_ref):
    chips, rows, width = parts_ref.shape
    tiles = width // LANES

    def tiled(x):
        return jnp.concatenate(
            [x[h : h + 1, q * LANES : (q + 1) * LANES] for h in range(rows) for q in range(tiles)], axis=0
        )

    row = lax.broadcasted_iota(jnp.int32, (8, chips * rows), 0)
    col = lax.broadcasted_iota(jnp.int32, (8, chips * rows), 1)
    pick = (col % rows == row).astype(BF16)
    grad = jnp.dot(pick, parts_ref[...].reshape(chips * rows, width), preferred_element_type=F32)[:rows]
    moment = tiled(carried_ref[...] + grad)
    table = table_ref[...]
    coeffs = lax.dot_general(moment, table, TURNED, precision=HIGHEST, preferred_element_type=F32)
    dense = jnp.where(tiled(mask_ref[...]) != 0.0, coeffs, 0.0)
    decoded = jnp.dot(dense, table, precision=HIGHEST, preferred_element_type=F32)
    kept = moment - decoded
    for peer in range(spread_ref.shape[0]):
        own = slice(peer % rows * tiles, (peer % rows + 1) * tiles)
        spread_ref[peer, :tiles, :] = decoded[own]
        spread_ref[peer, tiles:, :] = kept[own]


def finish_kernel(rep_ref, got_ref, kept_ref, update_ref):
    peers = got_ref.shape[0]
    tiles = got_ref.shape[1] // 2
    total = got_ref[0, :tiles, :]
    for peer in range(1, peers):
        total += got_ref[peer, :tiles, :]
    total = total / (peers // 2)
    kept = got_ref[2 * rep_ref[0]][tiles:, :] + got_ref[2 * rep_ref[0] + 1][tiles:, :]
    for q in range(tiles):
        lanes = slice(q * LANES, (q + 1) * LANES)
        update_ref[:, lanes] = total[q : q + 1]
        kept_ref[:, lanes] = kept[q : q + 1]


def local(acts, cotan, weight, momentum, select_ids):
    tok_rows, depth = acts.shape[1:]
    width = momentum.shape[2]
    segments = select_ids.shape[2]
    length = width // segments
    groups = lax.axis_size("rep")
    chips = lax.axis_size(CHIPS)
    cores = lax.axis_size("core")
    core = lax.axis_index("core")
    scale = 1.0 / math.sqrt(lax.axis_size(ROWS) * tok_rows)
    span = width // 2
    tiles = width // LANES

    sent = jnp.broadcast_to(weight.reshape(1, 2, span), (chips, 2, span))
    rows = lax.all_to_all(sent, CHIPS, 0, 0, tiled=True)
    whole = lax.all_gather(rows, "core", axis=0, tiled=False)
    term, dacts = pl.pallas_call(
        lambda *refs: backward_kernel(scale * 0.5, *refs),
        out_shape=(
            jax.ShapeDtypeStruct((chips, cores, width), BF16),
            jax.ShapeDtypeStruct((tok_rows, depth), BF16),
        ),
        in_specs=[ANY, ANY, ANY],
        out_specs=(VMEM, VMEM),
        scratch_shapes=[
            pltpu.VMEM((tok_rows, depth), BF16),
            pltpu.VMEM((2, tok_rows, span), BF16),
            pltpu.VMEM((cores, chips, 2, span), BF16),
            pltpu.SemaphoreType.DMA((4,)),
        ],
        compiler_params=params(56),
        cost_estimate=pl.CostEstimate(
            flops=6 * tok_rows * depth * width, bytes_accessed=3 * tok_rows * width, transcendentals=tok_rows * width
        ),
        name="backward",
    )(acts[0], cotan[0], whole)
    parts = lax.all_to_all(term, CHIPS, 0, 0, tiled=True)

    positions = jnp.arange(length)
    mask = jnp.any(select_ids[0, 0][..., None] == positions, axis=1).reshape(1, width).astype(F32)
    theirs = lax.ppermute(mask, "core", [(0, 1), (1, 0)])
    own = core == jnp.arange(cores)[:, None]
    masks = jnp.where(own, mask, theirs)
    carried = jnp.where(own, 0.9 * momentum[0], 0.0)
    table = jnp.kron(jnp.eye(LANES // length, dtype=F32), dct_table(length))
    spread = pl.pallas_call(
        select_kernel,
        out_shape=jax.ShapeDtypeStruct((groups * cores, 2 * tiles, LANES), F32),
        in_specs=[VMEM] * 4,
        out_specs=VMEM,
        compiler_params=params(8),
        name="select",
    )(parts, carried, masks, table)
    back = lax.all_to_all(spread, PEERS, 0, 0, tiled=True)
    new_momentum, update = pl.pallas_call(
        finish_kernel,
        out_shape=(jax.ShapeDtypeStruct((1, width), F32),) * 2,
        in_specs=[SMEM, VMEM],
        out_specs=(VMEM, VMEM),
        compiler_params=params(8),
        name="finish",
    )(lax.axis_index("rep").reshape(1).astype(jnp.int32), back)
    return (new_momentum[None], dacts[None], update)


def solution(mesh):
    shape = (8, 8, 2, mesh.shape["rep"])
    split = Mesh(mesh.devices.reshape(shape), (*ROWS, "rep"))
    placed = (
        P("rep", ROWS, None),
        P("rep", ROWS, None),
        P(ROWS, None),
        P("rep", ROWS, None),
        P("rep", ROWS, None, None),
    )
    return jax.shard_map(
        local,
        mesh=split,
        in_specs=placed,
        out_specs=(P("rep", ROWS, None), P("rep", ROWS, None), P(ROWS, None)),
        check_vma=False,
    )
```

```python
import math

import jax
import jax.numpy as jnp
import numpy as np
from jax import lax
from jax.experimental import pallas as pl
from jax.experimental.pallas import tpu as pltpu
from jax.sharding import Mesh
from jax.sharding import PartitionSpec as P

ROWS = ("y", "z", "core")
CHIPS = ("y", "z")
LANES = 128
HIGHEST = lax.Precision.HIGHEST
TURNED = (((1,), (1,)), ((), ()))
F32 = jnp.float32
BF16 = jnp.bfloat16
VMEM = pl.BlockSpec(memory_space=pltpu.VMEM)
SMEM = pl.BlockSpec(memory_space=pltpu.SMEM)


def params(mib):
    return pltpu.CompilerParams(vmem_limit_bytes=mib * 1024 * 1024)


def dct_table(length):
    index = np.arange(length)
    freq = index[:, None]
    factor = np.where(freq == 0, np.sqrt(1.0 / length), np.sqrt(2.0 / length))
    table = factor * np.cos(np.pi * (index[None, :] + 0.5) * freq / length)
    return np.kron(np.eye(LANES // length), table).astype(np.float32)


def grid_of(shape):
    return [lax.broadcasted_iota(jnp.int32, shape, dim) for dim in range(2)]


def send_kernel(row_ref, out_ref):
    row = row_ref[...]
    span = row.shape[1] // 2
    halves = jnp.concatenate([row[:, :span], row[:, span:]], axis=0)
    out_ref[...] = jnp.broadcast_to(halves[None], out_ref.shape)


def backward_kernel(scale, core_ref, acts_ref, cotan_ref, whole_ref, mine_ref, other_ref, dacts_ref):
    cores, chips, halves, span = whole_ref.shape
    depth = cores * chips
    held = whole_ref[...].reshape(depth * halves, span)
    row, col = grid_of((depth, depth * halves))
    out, own = grid_of((depth, depth))
    acts = acts_ref[...]
    total = None
    terms = [None, None]
    for half in range(halves):
        place = (((row % cores) * chips + row // cores) * halves + half == col).astype(BF16)
        slab = jnp.dot(place, held, preferred_element_type=F32).astype(BF16)
        mid = jnp.dot(acts, slab, preferred_element_type=F32)
        t = jnp.tanh(mid)
        slope = (1.0 + t) * (1.0 + mid * (1.0 - t))
        upstream = cotan_ref[:, half * span : (half + 1) * span]
        dpre = (upstream.astype(F32) * slope).astype(BF16)
        back = lax.dot_general(dpre, slab, TURNED, preferred_element_type=F32)
        total = back if total is None else total + back
        for side in range(2):
            core = core_ref[0] if side == 0 else 1 - core_ref[0]
            pick = jnp.where((out % halves == half) & (out // halves * cores + core == own), 1.0, 0.0).astype(BF16)
            lhs = lax.dot_general(pick, acts, TURNED, preferred_element_type=F32).astype(BF16)
            term = jnp.dot(lhs, dpre, preferred_element_type=F32)
            terms[side] = term if terms[side] is None else terms[side] + term
    mine_ref[...] = terms[0] * scale
    other_ref[...] = (terms[1] * scale).astype(BF16)
    dacts_ref[...] = total.astype(BF16)


def pair_kernel(core_ref, mine_ref, both_ref, out_ref):
    got = both_ref[1 - core_ref[0]].astype(F32)
    out_ref[...] = (mine_ref[...] + got).astype(BF16).reshape(out_ref.shape)


def select_kernel(parts_ref, carried_ref, mask_ref, table_ref, spread_ref, kept_ref):
    chips, halves, span = parts_ref.shape
    tiles = span // LANES
    row, col = grid_of((8, chips * halves))
    pick = (col % halves == row).astype(BF16)
    grad = jnp.dot(pick, parts_ref[...].reshape(chips * halves, span), preferred_element_type=F32)
    tiled = [grad[:halves, q * LANES : (q + 1) * LANES] for q in range(tiles)]
    moment = carried_ref[...] + jnp.concatenate(tiled, axis=0)
    table = table_ref[...]
    coeffs = lax.dot_general(moment, table, TURNED, precision=HIGHEST, preferred_element_type=F32)
    dense = jnp.where(mask_ref[...] != 0.0, coeffs, 0.0)
    decoded = jnp.dot(dense, table, precision=HIGHEST, preferred_element_type=F32)
    spread_ref[...] = jnp.broadcast_to(decoded[None], spread_ref.shape)
    kept_ref[...] = moment - decoded


def finish_kernel(got_ref, kept_ref, update_ref, momentum_ref):
    groups, rows, lanes = got_ref.shape
    total = got_ref[0]
    for group in range(1, groups):
        total += got_ref[group]
    total = total / groups
    kept = kept_ref[...]
    for r in range(rows):
        at = (r % 2 * (rows // 2) + r // 2) * lanes
        update_ref[:, at : at + lanes] = total[r : r + 1]
        momentum_ref[:, at : at + lanes] = kept[r : r + 1]


def local(acts, cotan, weight, momentum, select_ids):
    tok_rows, depth = acts.shape[1:]
    width = momentum.shape[2]
    length = width // select_ids.shape[2]
    groups = lax.axis_size("rep")
    chips = lax.axis_size(CHIPS)
    core = lax.axis_index("core").reshape(1).astype(jnp.int32)
    scale = 1.0 / math.sqrt(lax.axis_size(ROWS) * tok_rows)
    span = width // 2
    tiles = width // LANES
    table = dct_table(length)

    sent = pl.pallas_call(
        send_kernel,
        out_shape=jax.ShapeDtypeStruct((chips, 2, span), BF16),
        in_specs=[VMEM],
        out_specs=VMEM,
        compiler_params=params(8),
        name="send",
    )(weight)
    rows = lax.all_to_all(sent, CHIPS, 0, 0, tiled=True)
    carried = (0.9 * momentum).reshape(2, tiles // 2, LANES).transpose(1, 0, 2).reshape(tiles, LANES)
    ids = select_ids.reshape(2, tiles // 2, LANES // length, -1).transpose(1, 0, 2, 3)
    mask = jnp.any(ids[..., None] == jnp.arange(length), axis=3)
    mask = mask.reshape(tiles, LANES).astype(F32)
    half = jnp.asarray(0.5, BF16)
    rows, carried, mask, upstream, inputs = lax.optimization_barrier((rows, carried, mask, cotan[0] * half, acts[0] * half))
    whole = lax.all_gather(rows, "core", axis=0, tiled=False)
    mine, other, dacts = pl.pallas_call(
        lambda *refs: backward_kernel(scale * 2.0, *refs),
        out_shape=(
            jax.ShapeDtypeStruct((2 * chips, span), F32),
            jax.ShapeDtypeStruct((2 * chips, span), BF16),
            jax.ShapeDtypeStruct((tok_rows, depth), BF16),
        ),
        in_specs=[SMEM, VMEM, VMEM, VMEM],
        out_specs=(VMEM, VMEM, VMEM),
        compiler_params=params(32),
        cost_estimate=pl.CostEstimate(
            flops=6 * tok_rows * depth * width, bytes_accessed=3 * tok_rows * width, transcendentals=tok_rows * width
        ),
        name="backward",
    )(core, inputs, upstream, whole)
    both = lax.all_gather(other, "core", axis=0, tiled=False)
    chip_sum = pl.pallas_call(
        pair_kernel,
        out_shape=jax.ShapeDtypeStruct((chips, 2, span), BF16),
        in_specs=[SMEM, VMEM, VMEM],
        out_specs=VMEM,
        compiler_params=params(8),
        name="pair",
    )(core, mine, both)
    parts = lax.all_to_all(chip_sum, CHIPS, 0, 0, tiled=True)
    spread, kept = pl.pallas_call(
        select_kernel,
        out_shape=(
            jax.ShapeDtypeStruct((groups, tiles, LANES), F32),
            jax.ShapeDtypeStruct((tiles, LANES), F32),
        ),
        in_specs=[VMEM] * 4,
        out_specs=(VMEM, VMEM),
        compiler_params=params(8),
        name="select",
    )(parts, carried, mask, table)
    back = lax.all_to_all(spread, "rep", 0, 0, tiled=True)
    update, new_momentum = pl.pallas_call(
        finish_kernel,
        out_shape=(jax.ShapeDtypeStruct((1, width), F32),) * 2,
        in_specs=[VMEM, VMEM],
        out_specs=(VMEM, VMEM),
        compiler_params=params(8),
        name="finish",
    )(back, kept)
    return (new_momentum[None], dacts[None], update)


def solution(mesh):
    shape = (8, 8, 2, mesh.shape["rep"])
    split = Mesh(mesh.devices.reshape(shape), (*ROWS, "rep"))
    placed = (
        P("rep", ROWS, None),
        P("rep", ROWS, None),
        P(ROWS, None),
        P("rep", ROWS, None),
        P("rep", ROWS, None, None),
    )
    return jax.shard_map(
        local,
        mesh=split,
        in_specs=placed,
        out_specs=(P("rep", ROWS, None), P("rep", ROWS, None), P(ROWS, None)),
        check_vma=False,
    )
```

```python
import math

import jax
import jax.numpy as jnp
import numpy as np
from jax import lax
from jax.experimental import pallas as pl
from jax.experimental.pallas import tpu as pltpu
from jax.sharding import Mesh
from jax.sharding import PartitionSpec as P

ROWS = ("y", "z", "core")
CHIPS = ("y", "z")
LANES = 128
HIGHEST = lax.Precision.HIGHEST
TURNED = (((1,), (1,)), ((), ()))
F32 = jnp.float32
BF16 = jnp.bfloat16
VMEM = pl.BlockSpec(memory_space=pltpu.VMEM)
SMEM = pl.BlockSpec(memory_space=pltpu.SMEM)


def params(mib):
    return pltpu.CompilerParams(vmem_limit_bytes=mib * 1024 * 1024)


def dct_table(length):
    index = np.arange(length)
    freq = index[:, None]
    factor = np.where(freq == 0, np.sqrt(1.0 / length), np.sqrt(2.0 / length))
    table = factor * np.cos(np.pi * (index[None, :] + 0.5) * freq / length)
    return np.kron(np.eye(LANES // length), table).astype(np.float32)


def grid_of(shape):
    return [lax.broadcasted_iota(jnp.int32, shape, dim) for dim in range(2)]


def send_kernel(row_ref, out_ref):
    row = row_ref[...]
    span = row.shape[1] // 2
    halves = jnp.concatenate([row[:, :span], row[:, span:]], axis=0)
    out_ref[...] = jnp.broadcast_to(halves[None], out_ref.shape)


def backward_kernel(scale, core_ref, acts_ref, cotan_ref, whole_ref, mine_ref, other_ref, dacts_ref):
    cores, chips, halves, span = whole_ref.shape
    depth = cores * chips
    held = whole_ref[...].reshape(depth * halves, span)
    row, col = grid_of((depth, depth * halves))
    out, own = grid_of((cores * depth, depth))
    core = jnp.where(out < depth, core_ref[0], 1 - core_ref[0])
    out = out % depth
    acts = acts_ref[...]
    total = None
    terms = None
    for half in range(halves):
        place = (((row % cores) * chips + row // cores) * halves + half == col).astype(BF16)
        slab = jnp.dot(place, held, preferred_element_type=F32).astype(BF16)
        mid = jnp.dot(acts, slab, preferred_element_type=F32)
        t = jnp.tanh(mid)
        slope = (1.0 + t) * (1.0 + mid * (1.0 - t))
        upstream = cotan_ref[:, half * span : (half + 1) * span]
        dpre = (upstream.astype(F32) * slope).astype(BF16)
        back = lax.dot_general(dpre, slab, TURNED, preferred_element_type=F32)
        total = back if total is None else total + back
        pick = jnp.where((out % halves == half) & (out // halves * cores + core == own), 1.0, 0.0).astype(BF16)
        lhs = lax.dot_general(pick, acts, TURNED, preferred_element_type=F32).astype(BF16)
        term = jnp.dot(lhs, dpre, preferred_element_type=F32)
        terms = term if terms is None else terms + term
    mine_ref[...] = terms[:depth] * scale
    other_ref[...] = (terms[depth:] * scale).astype(BF16)
    dacts_ref[...] = total.astype(BF16)


def pair_kernel(core_ref, mine_ref, both_ref, out_ref):
    got = both_ref[1 - core_ref[0]].astype(F32)
    out_ref[...] = (mine_ref[...] + got).astype(BF16).reshape(out_ref.shape)


def select_kernel(parts_ref, carried_ref, mask_ref, table_ref, spread_ref, kept_ref):
    chips, halves, span = parts_ref.shape
    tiles = span // LANES
    row, col = grid_of((8, chips * halves))
    pick = (col % halves == row).astype(BF16)
    grad = jnp.dot(pick, parts_ref[...].reshape(chips * halves, span), preferred_element_type=F32)
    tiled = [grad[:halves, q * LANES : (q + 1) * LANES] for q in range(tiles)]
    moment = carried_ref[...] + jnp.concatenate(tiled, axis=0)
    table = table_ref[...]
    coeffs = lax.dot_general(moment, table, TURNED, precision=HIGHEST, preferred_element_type=F32)
    dense = jnp.where(mask_ref[...] != 0.0, coeffs, 0.0)
    decoded = jnp.dot(dense, table, precision=HIGHEST, preferred_element_type=F32)
    spread_ref[...] = jnp.broadcast_to(decoded.astype(BF16)[None], spread_ref.shape)
    kept_ref[...] = moment - decoded


def finish_kernel(got_ref, kept_ref, held_ref, update_ref, momentum_ref, dacts_ref):
    dacts_ref[...] = held_ref[...]
    groups, rows, lanes = got_ref.shape
    total = got_ref[0].astype(F32)
    for group in range(1, groups):
        total += got_ref[group].astype(F32)
    total = total / groups
    kept = kept_ref[...]
    for r in range(rows):
        at = (r % 2 * (rows // 2) + r // 2) * lanes
        update_ref[:, at : at + lanes] = total[r : r + 1]
        momentum_ref[:, at : at + lanes] = kept[r : r + 1]


def local(acts, cotan, weight, momentum, select_ids):
    tok_rows, depth = acts.shape[1:]
    width = momentum.shape[2]
    length = width // select_ids.shape[2]
    groups = lax.axis_size("rep")
    chips = lax.axis_size(CHIPS)
    core = lax.axis_index("core").reshape(1).astype(jnp.int32)
    scale = 1.0 / math.sqrt(lax.axis_size(ROWS) * tok_rows)
    span = width // 2
    tiles = width // LANES
    table = dct_table(length)

    sent = pl.pallas_call(
        send_kernel,
        out_shape=jax.ShapeDtypeStruct((chips, 2, span), BF16),
        in_specs=[VMEM],
        out_specs=VMEM,
        compiler_params=params(8),
        name="send",
    )(weight)
    rows = lax.all_to_all(sent, CHIPS, 0, 0, tiled=True)
    carried = (0.9 * momentum).reshape(2, tiles // 2, LANES).transpose(1, 0, 2).reshape(tiles, LANES)
    ids = select_ids.reshape(2, tiles // 2, LANES // length, -1).transpose(1, 0, 2, 3)
    mask = jnp.any(ids[..., None] == jnp.arange(length), axis=3)
    mask = mask.reshape(tiles, LANES).astype(F32)
    half = jnp.asarray(0.5, BF16)
    rows, carried, mask, upstream, inputs = lax.optimization_barrier((rows, carried, mask, cotan[0] * half, acts[0] * half))
    whole = lax.all_gather(rows, "core", axis=0, tiled=False)
    mine, other, held = pl.pallas_call(
        lambda *refs: backward_kernel(scale * 2.0, *refs),
        out_shape=(
            jax.ShapeDtypeStruct((2 * chips, span), F32),
            jax.ShapeDtypeStruct((2 * chips, span), BF16),
            jax.ShapeDtypeStruct((tok_rows, depth), BF16),
        ),
        in_specs=[SMEM, VMEM, VMEM, VMEM],
        out_specs=(VMEM, VMEM, VMEM),
        compiler_params=params(32),
        cost_estimate=pl.CostEstimate(
            flops=6 * tok_rows * depth * width, bytes_accessed=3 * tok_rows * width, transcendentals=tok_rows * width
        ),
        name="backward",
    )(core, inputs, upstream, whole)
    both = lax.all_gather(other, "core", axis=0, tiled=False)
    chip_sum = pl.pallas_call(
        pair_kernel,
        out_shape=jax.ShapeDtypeStruct((chips, 2, span), BF16),
        in_specs=[SMEM, VMEM, VMEM],
        out_specs=VMEM,
        compiler_params=params(8),
        name="pair",
    )(core, mine, both)
    parts = lax.all_to_all(chip_sum, CHIPS, 0, 0, tiled=True)
    spread, kept = pl.pallas_call(
        select_kernel,
        out_shape=(
            jax.ShapeDtypeStruct((groups, tiles, LANES), BF16),
            jax.ShapeDtypeStruct((tiles, LANES), F32),
        ),
        in_specs=[VMEM] * 4,
        out_specs=(VMEM, VMEM),
        compiler_params=params(8),
        name="select",
    )(parts, carried, mask, table)
    back = lax.all_to_all(spread, "rep", 0, 0, tiled=True)
    update, new_momentum, dacts = pl.pallas_call(
        finish_kernel,
        out_shape=(
            jax.ShapeDtypeStruct((1, width), F32),
            jax.ShapeDtypeStruct((1, width), F32),
            jax.ShapeDtypeStruct((tok_rows, depth), BF16),
        ),
        in_specs=[VMEM, VMEM, VMEM],
        out_specs=(VMEM, VMEM, VMEM),
        compiler_params=params(8),
        name="finish",
    )(back, kept, held)
    return (new_momentum[None], dacts[None], update)


def solution(mesh):
    shape = (8, 8, 2, mesh.shape["rep"])
    split = Mesh(mesh.devices.reshape(shape), (*ROWS, "rep"))
    placed = (
        P("rep", ROWS, None),
        P("rep", ROWS, None),
        P(ROWS, None),
        P("rep", ROWS, None),
        P("rep", ROWS, None, None),
    )
    return jax.shard_map(
        local,
        mesh=split,
        in_specs=placed,
        out_specs=(P("rep", ROWS, None), P("rep", ROWS, None), P(ROWS, None)),
        check_vma=False,
    )
```

```python
import math

import jax
import jax.numpy as jnp
import numpy as np
from jax import lax
from jax.experimental import pallas as pl
from jax.experimental.pallas import tpu as pltpu
from jax.sharding import Mesh
from jax.sharding import PartitionSpec as P

ROWS = ("y", "z", "core")
CHIPS = ("y", "z")
LANES = 128
HIGHEST = lax.Precision.HIGHEST
TURNED = (((1,), (1,)), ((), ()))
F32 = jnp.float32
BF16 = jnp.bfloat16
VMEM = pl.BlockSpec(memory_space=pltpu.VMEM)
SMEM = pl.BlockSpec(memory_space=pltpu.SMEM)


def params(mib):
    return pltpu.CompilerParams(vmem_limit_bytes=mib * 1024 * 1024)


def dct_table(length):
    index = np.arange(length)
    freq = index[:, None]
    factor = np.where(freq == 0, np.sqrt(1.0 / length), np.sqrt(2.0 / length))
    table = factor * np.cos(np.pi * (index[None, :] + 0.5) * freq / length)
    return np.kron(np.eye(LANES // length), table).astype(np.float32)


def grid_of(shape):
    return [lax.broadcasted_iota(jnp.int32, shape, dim) for dim in range(2)]


def send_kernel(core_ref, pair_ref, out_ref):
    cores, span = out_ref.shape[1:]
    half = pl.ds(pl.multiple_of(core_ref[0] * span, LANES), span)
    rows = jnp.concatenate([pair_ref[c, :, half] for c in range(cores)], axis=0)
    out_ref[...] = jnp.broadcast_to(rows[None], out_ref.shape)


def unpack_kernel(slab_ref, out_ref):
    out_ref[...] = slab_ref[...].reshape(out_ref.shape)


def backward_kernel(scale, acts_ref, cotan_ref, got_ref, slab_ref, term_ref, mine_ref, theirs_ref):
    depth, span = slab_ref.shape
    slab = slab_ref[...]
    total = None
    for side, back_ref in enumerate((mine_ref, theirs_ref)):
        acts = acts_ref[...] if side == 0 else got_ref[:, span:]
        upstream = cotan_ref[...] if side == 0 else got_ref[:, :span]
        mid = jnp.dot(acts, slab, preferred_element_type=F32)
        t = jnp.tanh(mid)
        slope = (1.0 + t) * (1.0 + mid * (1.0 - t))
        dpre = (upstream.astype(F32) * slope).astype(BF16)
        back_ref[...] = lax.dot_general(dpre, slab, TURNED, preferred_element_type=F32)
        term = jnp.dot(acts.T, dpre, preferred_element_type=F32)
        total = term if total is None else total + term
    term_ref[...] = (total * scale).astype(BF16).reshape(term_ref.shape)


def sum_kernel(core_ref, parts_ref, own_ref, other_ref):
    chips, rows, span = parts_ref.shape
    row, col = grid_of((8, chips * rows))
    wanted = jnp.where(row == 0, core_ref[0], 1 - core_ref[0])
    pick = jnp.where(col % rows == wanted, 1.0, 0.0).astype(BF16)
    grad = jnp.dot(pick, parts_ref[...].reshape(chips * rows, span), preferred_element_type=F32)
    own_ref[...] = grad[:1]
    other_ref[...] = grad[1:2]


def select_kernel(core_ref, own_ref, both_ref, carried_ref, mask_ref, table_ref, spread_ref, kept_ref):
    span = own_ref.shape[1]
    tiles = span // LANES
    own, got = own_ref[...], both_ref[1 - core_ref[0]]
    first = core_ref[0] == 0
    grad = jnp.concatenate([jnp.where(first, own, got), jnp.where(first, got, own)], axis=0)
    tiled = [grad[:, q * LANES : (q + 1) * LANES] for q in range(tiles)]
    moment = carried_ref[...] + jnp.concatenate(tiled, axis=0)
    table = table_ref[...]
    coeffs = lax.dot_general(moment, table, TURNED, precision=HIGHEST, preferred_element_type=F32)
    dense = jnp.where(mask_ref[...] != 0.0, coeffs, 0.0)
    decoded = jnp.dot(dense, table, precision=HIGHEST, preferred_element_type=F32)
    spread_ref[...] = jnp.broadcast_to(decoded.astype(BF16)[None], spread_ref.shape)
    kept_ref[...] = moment - decoded


def finish_kernel(got_ref, kept_ref, mine_ref, theirs_ref, update_ref, momentum_ref, dacts_ref):
    dacts_ref[...] = (mine_ref[...] + theirs_ref[...]).astype(BF16)
    groups, rows, lanes = got_ref.shape
    total = got_ref[0].astype(F32)
    for group in range(1, groups):
        total += got_ref[group].astype(F32)
    total = total / groups
    kept = kept_ref[...]
    for r in range(rows):
        at = (r % 2 * (rows // 2) + r // 2) * lanes
        update_ref[:, at : at + lanes] = total[r : r + 1]
        momentum_ref[:, at : at + lanes] = kept[r : r + 1]


def other_core(x):
    return lax.ppermute(x, "core", [(0, 1), (1, 0)])


def local(acts, cotan, weight, momentum, select_ids):
    tok_rows, depth = acts.shape[1:]
    width = momentum.shape[2]
    length = width // select_ids.shape[2]
    groups = lax.axis_size("rep")
    chips = lax.axis_size(CHIPS)
    core = lax.axis_index("core").reshape(1).astype(jnp.int32)
    scale = 1.0 / math.sqrt(lax.axis_size(ROWS) * tok_rows)
    span = width // 2
    tiles = width // LANES
    table = dct_table(length)

    pair = lax.all_gather(weight, "core", axis=0, tiled=False)
    sent = pl.pallas_call(
        send_kernel,
        out_shape=jax.ShapeDtypeStruct((chips, 2, span), BF16),
        in_specs=[SMEM, VMEM],
        out_specs=VMEM,
        compiler_params=params(8),
        name="send",
    )(core, pair)
    slab = lax.all_to_all(sent, CHIPS, 0, 0, tiled=True)
    carried = (0.9 * momentum).reshape(2, tiles // 2, LANES).transpose(1, 0, 2).reshape(tiles, LANES)
    ids = select_ids.reshape(2, tiles // 2, LANES // length, -1).transpose(1, 0, 2, 3)
    mask = jnp.any(ids[..., None] == jnp.arange(length), axis=3)
    mask = mask.reshape(tiles, LANES).astype(F32)
    half = jnp.asarray(0.5, BF16)
    first = core[0] == 0
    low, high = cotan[0][:, :span] * half, cotan[0][:, span:] * half
    inputs = acts[0] * half
    got = other_core(jnp.concatenate([jnp.where(first, high, low), inputs], axis=1))
    slab, carried, mask, upstream, inputs = lax.optimization_barrier(
        (slab, carried, mask, jnp.where(first, low, high), inputs)
    )
    slab = pl.pallas_call(
        unpack_kernel,
        out_shape=jax.ShapeDtypeStruct((depth, span), BF16),
        in_specs=[VMEM],
        out_specs=VMEM,
        compiler_params=params(8),
        cost_estimate=pl.CostEstimate(flops=1 << 36, bytes_accessed=0, transcendentals=0),
        name="unpack",
    )(slab)
    term, mine, theirs = pl.pallas_call(
        lambda *refs: backward_kernel(scale * 2.0, *refs),
        out_shape=(
            jax.ShapeDtypeStruct((chips, 2, span), BF16),
            jax.ShapeDtypeStruct((tok_rows, depth), F32),
            jax.ShapeDtypeStruct((tok_rows, depth), F32),
        ),
        in_specs=[VMEM] * 4,
        out_specs=(VMEM,) * 3,
        compiler_params=params(32),
        cost_estimate=pl.CostEstimate(
            flops=6 * tok_rows * depth * width, bytes_accessed=3 * tok_rows * width, transcendentals=tok_rows * width
        ),
        name="backward",
    )(inputs, upstream, got, slab)
    parts = lax.all_to_all(term, CHIPS, 0, 0, tiled=True)
    parts, mine, theirs = lax.optimization_barrier((parts, mine, other_core(theirs)))
    own, other = pl.pallas_call(
        sum_kernel,
        out_shape=(jax.ShapeDtypeStruct((1, span), F32),) * 2,
        in_specs=[SMEM, VMEM],
        out_specs=(VMEM, VMEM),
        compiler_params=params(8),
        name="sum",
    )(core, parts)
    both = lax.all_gather(other, "core", axis=0, tiled=False)
    spread, kept = pl.pallas_call(
        select_kernel,
        out_shape=(
            jax.ShapeDtypeStruct((groups, tiles, LANES), BF16),
            jax.ShapeDtypeStruct((tiles, LANES), F32),
        ),
        in_specs=[SMEM] + [VMEM] * 5,
        out_specs=(VMEM, VMEM),
        compiler_params=params(8),
        name="select",
    )(core, own, both, carried, mask, table)
    back = lax.all_to_all(spread, "rep", 0, 0, tiled=True)
    update, new_momentum, dacts = pl.pallas_call(
        finish_kernel,
        out_shape=(
            jax.ShapeDtypeStruct((1, width), F32),
            jax.ShapeDtypeStruct((1, width), F32),
            jax.ShapeDtypeStruct((tok_rows, depth), BF16),
        ),
        in_specs=[VMEM] * 4,
        out_specs=(VMEM, VMEM, VMEM),
        compiler_params=params(8),
        name="finish",
    )(back, kept, mine, theirs)
    return (new_momentum[None], dacts[None], update)


def solution(mesh):
    shape = (8, 8, 2, mesh.shape["rep"])
    split = Mesh(mesh.devices.reshape(shape), (*ROWS, "rep"))
    placed = (
        P("rep", ROWS, None),
        P("rep", ROWS, None),
        P(ROWS, None),
        P("rep", ROWS, None),
        P("rep", ROWS, None, None),
    )
    return jax.shard_map(
        local,
        mesh=split,
        in_specs=placed,
        out_specs=(P("rep", ROWS, None), P("rep", ROWS, None), P(ROWS, None)),
        check_vma=False,
    )
```

```python
import math

import jax
import jax.numpy as jnp
import numpy as np
from jax import lax
from jax.experimental import pallas as pl
from jax.experimental.pallas import tpu as pltpu
from jax.sharding import Mesh
from jax.sharding import PartitionSpec as P

ROWS = ("y", "z", "core")
CHIPS = ("y", "z")
LANES = 128
HIGHEST = lax.Precision.HIGHEST
TURNED = (((1,), (1,)), ((), ()))
F32 = jnp.float32
BF16 = jnp.bfloat16
VMEM = pl.BlockSpec(memory_space=pltpu.VMEM)
SMEM = pl.BlockSpec(memory_space=pltpu.SMEM)


def params(mib):
    return pltpu.CompilerParams(vmem_limit_bytes=mib * 1024 * 1024)


def dct_table(length):
    index = np.arange(length)
    freq = index[:, None]
    factor = np.where(freq == 0, np.sqrt(1.0 / length), np.sqrt(2.0 / length))
    table = factor * np.cos(np.pi * (index[None, :] + 0.5) * freq / length)
    return np.kron(np.eye(LANES // length), table).astype(np.float32)


def grid_of(shape):
    return [lax.broadcasted_iota(jnp.int32, shape, dim) for dim in range(2)]


def send_kernel(core_ref, pair_ref, out_ref):
    cores, span = out_ref.shape[1:]
    half = pl.ds(pl.multiple_of(core_ref[0] * span, LANES), span)
    rows = jnp.concatenate([pair_ref[c, :, half] for c in range(cores)], axis=0)
    out_ref[...] = jnp.broadcast_to(rows[None], out_ref.shape)


def unpack_kernel(slab_ref, out_ref):
    out_ref[...] = slab_ref[...].reshape(out_ref.shape)


def backward_kernel(scale, acts_ref, cotan_ref, got_ref, slab_ref, term_ref, mine_ref, theirs_ref):
    depth, span = slab_ref.shape
    slab = slab_ref[...]
    total = None
    for side, back_ref in enumerate((mine_ref, theirs_ref)):
        acts = acts_ref[...] if side == 0 else got_ref[:, span:]
        upstream = cotan_ref[...] if side == 0 else got_ref[:, :span]
        mid = jnp.dot(acts, slab, preferred_element_type=F32)
        t = jnp.tanh(mid)
        slope = (1.0 + t) * (1.0 + mid * (1.0 - t))
        dpre = (upstream.astype(F32) * slope).astype(BF16)
        back_ref[...] = lax.dot_general(dpre, slab, TURNED, preferred_element_type=F32)
        term = jnp.dot(acts.T, dpre, preferred_element_type=F32)
        total = term if total is None else total + term
    term_ref[...] = (total * scale).astype(BF16).reshape(term_ref.shape)


def sum_kernel(core_ref, parts_ref, theirs_ref, own_ref, out_ref):
    chips, rows, span = parts_ref.shape
    toks = theirs_ref.shape[0]
    row, col = grid_of((8, chips * rows))
    wanted = jnp.where(row == 0, core_ref[0], 1 - core_ref[0])
    pick = jnp.where(col % rows == wanted, 1.0, 0.0).astype(BF16)
    grad = jnp.dot(pick, parts_ref[...].reshape(chips * rows, span), preferred_element_type=F32)
    own_ref[...] = grad[:1]
    out_ref[:toks, :] = theirs_ref[...]
    tiles = span // LANES
    pad = jnp.zeros((out_ref.shape[0] - toks - tiles, LANES), F32)
    other = [grad[1:2, q * LANES : (q + 1) * LANES] for q in range(tiles)]
    out_ref[toks:, :] = jnp.concatenate([*other, pad], axis=0)


def select_kernel(toks, core_ref, own_ref, both_ref, carried_ref, mask_ref, table_ref, spread_ref, kept_ref):
    tiles = own_ref.shape[1] // LANES
    got = both_ref[1 - core_ref[0], toks:, :]
    first = core_ref[0] == 0
    tiled = []
    for q in range(tiles):
        here, there = own_ref[:, q * LANES : (q + 1) * LANES], got[q : q + 1]
        tiled += [jnp.where(first, here, there), jnp.where(first, there, here)]
    moment = carried_ref[...] + jnp.concatenate(tiled, axis=0)
    table = table_ref[...]
    coeffs = lax.dot_general(moment, table, TURNED, precision=HIGHEST, preferred_element_type=F32)
    dense = jnp.where(mask_ref[...] != 0.0, coeffs, 0.0)
    decoded = jnp.dot(dense, table, precision=HIGHEST, preferred_element_type=F32)
    spread_ref[...] = jnp.broadcast_to(decoded.astype(BF16)[None], spread_ref.shape)
    kept_ref[...] = moment - decoded


def finish_kernel(core_ref, got_ref, kept_ref, mine_ref, both_ref, update_ref, momentum_ref, dacts_ref):
    theirs = both_ref[1 - core_ref[0], : dacts_ref.shape[0], :]
    dacts_ref[...] = (mine_ref[...] + theirs).astype(BF16)
    groups, rows, lanes = got_ref.shape
    total = got_ref[0].astype(F32)
    for group in range(1, groups):
        total += got_ref[group].astype(F32)
    total = total / groups
    kept = kept_ref[...]
    for r in range(rows):
        at = (r % 2 * (rows // 2) + r // 2) * lanes
        update_ref[:, at : at + lanes] = total[r : r + 1]
        momentum_ref[:, at : at + lanes] = kept[r : r + 1]


def other_core(x):
    return lax.ppermute(x, "core", [(0, 1), (1, 0)])


def local(acts, cotan, weight, momentum, select_ids):
    tok_rows, depth = acts.shape[1:]
    width = momentum.shape[2]
    length = width // select_ids.shape[2]
    groups = lax.axis_size("rep")
    chips = lax.axis_size(CHIPS)
    core = lax.axis_index("core").reshape(1).astype(jnp.int32)
    scale = 1.0 / math.sqrt(lax.axis_size(ROWS) * tok_rows)
    span = width // 2
    tiles = width // LANES
    table = dct_table(length)

    pair = lax.all_gather(weight, "core", axis=0, tiled=False)
    sent = pl.pallas_call(
        send_kernel,
        out_shape=jax.ShapeDtypeStruct((chips, 2, span), BF16),
        in_specs=[SMEM, VMEM],
        out_specs=VMEM,
        compiler_params=params(8),
        name="send",
    )(core, pair)
    slab = lax.all_to_all(sent, CHIPS, 0, 0, tiled=True)
    carried = (0.9 * momentum).reshape(2, tiles // 2, LANES).transpose(1, 0, 2).reshape(tiles, LANES)
    ids = select_ids.reshape(2, tiles // 2, LANES // length, -1).transpose(1, 0, 2, 3)
    mask = jnp.any(ids[..., None] == jnp.arange(length), axis=3)
    mask = mask.reshape(tiles, LANES).astype(F32)
    half = jnp.asarray(0.5, BF16)
    first = core[0] == 0
    low, high = cotan[0][:, :span] * half, cotan[0][:, span:] * half
    inputs = acts[0] * half
    got = other_core(jnp.concatenate([jnp.where(first, high, low), inputs], axis=1))
    slab, carried, mask, upstream, inputs = lax.optimization_barrier(
        (slab, carried, mask, jnp.where(first, low, high), inputs)
    )
    slab = pl.pallas_call(
        unpack_kernel,
        out_shape=jax.ShapeDtypeStruct((depth, span), BF16),
        in_specs=[VMEM],
        out_specs=VMEM,
        compiler_params=params(8),
        cost_estimate=pl.CostEstimate(flops=1 << 36, bytes_accessed=0, transcendentals=0),
        name="unpack",
    )(slab)
    term, mine, theirs = pl.pallas_call(
        lambda *refs: backward_kernel(scale * 2.0, *refs),
        out_shape=(
            jax.ShapeDtypeStruct((chips, 2, span), BF16),
            jax.ShapeDtypeStruct((tok_rows, depth), F32),
            jax.ShapeDtypeStruct((tok_rows, depth), F32),
        ),
        in_specs=[VMEM] * 4,
        out_specs=(VMEM,) * 3,
        compiler_params=params(32),
        cost_estimate=pl.CostEstimate(
            flops=6 * tok_rows * depth * width, bytes_accessed=3 * tok_rows * width, transcendentals=tok_rows * width
        ),
        name="backward",
    )(inputs, upstream, got, slab)
    parts = lax.all_to_all(term, CHIPS, 0, 0, tiled=True)
    own, other = pl.pallas_call(
        sum_kernel,
        out_shape=(
            jax.ShapeDtypeStruct((1, span), F32),
            jax.ShapeDtypeStruct((tok_rows + 16, LANES), F32),
        ),
        in_specs=[SMEM, VMEM, VMEM],
        out_specs=(VMEM, VMEM),
        compiler_params=params(8),
        name="sum",
    )(core, parts, theirs)
    both = lax.all_gather(other, "core", axis=0, tiled=False)
    spread, kept = pl.pallas_call(
        lambda *refs: select_kernel(tok_rows, *refs),
        out_shape=(
            jax.ShapeDtypeStruct((groups, tiles, LANES), BF16),
            jax.ShapeDtypeStruct((tiles, LANES), F32),
        ),
        in_specs=[SMEM] + [VMEM] * 5,
        out_specs=(VMEM, VMEM),
        compiler_params=params(8),
        name="select",
    )(core, own, both, carried, mask, table)
    back = lax.all_to_all(spread, "rep", 0, 0, tiled=True)
    update, new_momentum, dacts = pl.pallas_call(
        finish_kernel,
        out_shape=(
            jax.ShapeDtypeStruct((1, width), F32),
            jax.ShapeDtypeStruct((1, width), F32),
            jax.ShapeDtypeStruct((tok_rows, depth), BF16),
        ),
        in_specs=[SMEM] + [VMEM] * 4,
        out_specs=(VMEM, VMEM, VMEM),
        compiler_params=params(8),
        name="finish",
    )(core, back, kept, mine, both)
    return (new_momentum[None], dacts[None], update)


def solution(mesh):
    shape = (8, 8, 2, mesh.shape["rep"])
    split = Mesh(mesh.devices.reshape(shape), (*ROWS, "rep"))
    placed = (
        P("rep", ROWS, None),
        P("rep", ROWS, None),
        P(ROWS, None),
        P("rep", ROWS, None),
        P("rep", ROWS, None, None),
    )
    return jax.shard_map(
        local,
        mesh=split,
        in_specs=placed,
        out_specs=(P("rep", ROWS, None), P("rep", ROWS, None), P(ROWS, None)),
        check_vma=False,
    )
```

```python
import math

import jax
import jax.numpy as jnp
import numpy as np
from jax import lax
from jax.experimental import pallas as pl
from jax.experimental.pallas import tpu as pltpu
from jax.sharding import Mesh
from jax.sharding import PartitionSpec as P

ROWS = ("chip", "core")
LANES = 128
HIGHEST = lax.Precision.HIGHEST
TURNED = (((1,), (1,)), ((), ()))
F32 = jnp.float32
BF16 = jnp.bfloat16
VMEM = pl.BlockSpec(memory_space=pltpu.VMEM)
SMEM = pl.BlockSpec(memory_space=pltpu.SMEM)


def params(mib):
    return pltpu.CompilerParams(vmem_limit_bytes=mib * 1024 * 1024)


def dct_table(length):
    index = np.arange(length)
    freq = index[:, None]
    factor = np.where(freq == 0, np.sqrt(1.0 / length), np.sqrt(2.0 / length))
    table = factor * np.cos(np.pi * (index[None, :] + 0.5) * freq / length)
    return np.kron(np.eye(LANES // length), table).astype(np.float32)


def half_placed(order):
    count = 2 * len(order)
    table = np.zeros((count, count), np.float32)
    for i, chip in enumerate(order):
        for c in range(2):
            table[2 * chip + c, 2 * i + c] = 0.5
    return table.astype(BF16)


def grid_of(shape):
    return [lax.broadcasted_iota(jnp.int32, shape, dim) for dim in range(2)]


def send_kernel(core_ref, pair_ref, out_ref):
    cores, span = out_ref.shape[1:]
    half = pl.ds(pl.multiple_of(core_ref[0] * span, LANES), span)
    rows = jnp.concatenate([pair_ref[c, :, half] for c in range(cores)], axis=0)
    out_ref[...] = jnp.broadcast_to(rows[None], out_ref.shape)


def unpack_kernel(slab_ref, out_ref):
    out_ref[...] = slab_ref[...].reshape(out_ref.shape)


def backward_kernel(scale, acts_ref, cotan_ref, got_ref, slab_ref, term_ref, mine_ref, theirs_ref):
    depth, span = slab_ref.shape
    slab = slab_ref[...]
    total = None
    for side, back_ref in enumerate((mine_ref, theirs_ref)):
        acts = acts_ref[...] if side == 0 else got_ref[:, span:]
        upstream = cotan_ref[...] if side == 0 else got_ref[:, :span]
        mid = jnp.dot(acts, slab, preferred_element_type=F32)
        t = jnp.tanh(mid)
        slope = (1.0 + t) * (1.0 + mid * (1.0 - t))
        dpre = (upstream.astype(F32) * slope).astype(BF16)
        back_ref[...] = lax.dot_general(dpre, slab, TURNED, preferred_element_type=F32)
        term = jnp.dot(acts.T, dpre, preferred_element_type=F32)
        total = term if total is None else total + term
    term_ref[...] = (total * scale).astype(BF16).reshape(term_ref.shape)


def sum_kernel(core_ref, parts_ref, theirs_ref, own_ref, out_ref):
    chips, rows, span = parts_ref.shape
    toks = theirs_ref.shape[0]
    row, col = grid_of((8, chips * rows))
    wanted = jnp.where(row == 0, core_ref[0], 1 - core_ref[0])
    pick = jnp.where(col % rows == wanted, 1.0, 0.0).astype(BF16)
    grad = jnp.dot(pick, parts_ref[...].reshape(chips * rows, span), preferred_element_type=F32)
    own_ref[...] = grad[:1]
    out_ref[:toks, :] = theirs_ref[...]
    tiles = span // LANES
    pad = jnp.zeros((out_ref.shape[0] - toks - tiles, LANES), F32)
    other = [grad[1:2, q * LANES : (q + 1) * LANES] for q in range(tiles)]
    out_ref[toks:, :] = jnp.concatenate([*other, pad], axis=0)


def select_kernel(toks, core_ref, own_ref, both_ref, carried_ref, mask_ref, table_ref, spread_ref, kept_ref):
    tiles = own_ref.shape[1] // LANES
    got = both_ref[1 - core_ref[0], toks:, :]
    first = core_ref[0] == 0
    tiled = []
    for q in range(tiles):
        here, there = own_ref[:, q * LANES : (q + 1) * LANES], got[q : q + 1]
        tiled += [jnp.where(first, here, there), jnp.where(first, there, here)]
    moment = carried_ref[...] + jnp.concatenate(tiled, axis=0)
    table = table_ref[...]
    coeffs = lax.dot_general(moment, table, TURNED, precision=HIGHEST, preferred_element_type=F32)
    dense = jnp.where(mask_ref[...] != 0.0, coeffs, 0.0)
    decoded = jnp.dot(dense, table, precision=HIGHEST, preferred_element_type=F32)
    spread_ref[...] = jnp.broadcast_to(decoded.astype(BF16)[None], spread_ref.shape)
    kept_ref[...] = moment - decoded


def finish_kernel(core_ref, got_ref, kept_ref, mine_ref, both_ref, place_ref, update_ref, momentum_ref, dacts_ref):
    theirs = both_ref[1 - core_ref[0], : dacts_ref.shape[0], :]
    dacts = (mine_ref[...] + theirs).astype(BF16)
    dacts_ref[...] = (lax.dot_general(dacts, place_ref[...], TURNED, preferred_element_type=F32) * 2.0).astype(BF16)
    groups, rows, lanes = got_ref.shape
    total = got_ref[0].astype(F32)
    for group in range(1, groups):
        total += got_ref[group].astype(F32)
    total = total / groups
    kept = kept_ref[...]
    for r in range(rows):
        at = (r % 2 * (rows // 2) + r // 2) * lanes
        update_ref[:, at : at + lanes] = total[r : r + 1]
        momentum_ref[:, at : at + lanes] = kept[r : r + 1]


def other_core(x):
    return lax.ppermute(x, "core", [(0, 1), (1, 0)])


def local(acts, cotan, weight, momentum, select_ids):
    tok_rows, depth = acts.shape[1:]
    width = momentum.shape[2]
    length = width // select_ids.shape[2]
    groups = lax.axis_size("rep")
    chips = lax.axis_size("chip")
    order = list(range(chips))[::-1]
    place = half_placed(order)
    middle_out = sorted(range(groups), key=lambda g: (abs(g - groups // 2), g))
    core = lax.axis_index("core").reshape(1).astype(jnp.int32)
    scale = 1.0 / math.sqrt(lax.axis_size(ROWS) * tok_rows)
    span = width // 2
    tiles = width // LANES
    table = dct_table(length)

    pair = lax.all_gather(weight, "core", axis=0, tiled=False)
    sent = pl.pallas_call(
        send_kernel,
        out_shape=jax.ShapeDtypeStruct((chips, 2, span), BF16),
        in_specs=[SMEM, VMEM],
        out_specs=VMEM,
        compiler_params=params(8),
        name="send",
    )(core, pair)
    slab = lax.all_to_all(sent, "chip", 0, 0, tiled=True, axis_index_groups=[order])
    carried = (0.9 * momentum).reshape(2, tiles // 2, LANES).transpose(1, 0, 2).reshape(tiles, LANES)
    ids = select_ids.reshape(2, tiles // 2, LANES // length, -1).transpose(1, 0, 2, 3)
    mask = jnp.any(ids[..., None] == jnp.arange(length), axis=3)
    mask = mask.reshape(tiles, LANES).astype(F32)
    half = jnp.asarray(0.5, BF16)
    first = core[0] == 0
    low, high = cotan[0][:, :span] * half, cotan[0][:, span:] * half
    inputs = jnp.dot(acts[0], place, preferred_element_type=F32).astype(BF16)
    got = other_core(jnp.concatenate([jnp.where(first, high, low), inputs], axis=1))
    slab, carried, mask, upstream, inputs = lax.optimization_barrier(
        (slab, carried, mask, jnp.where(first, low, high), inputs)
    )
    slab = pl.pallas_call(
        unpack_kernel,
        out_shape=jax.ShapeDtypeStruct((depth, span), BF16),
        in_specs=[VMEM],
        out_specs=VMEM,
        compiler_params=params(8),
        cost_estimate=pl.CostEstimate(flops=1 << 36, bytes_accessed=0, transcendentals=0),
        name="unpack",
    )(slab)
    term, mine, theirs = pl.pallas_call(
        lambda *refs: backward_kernel(scale * 2.0, *refs),
        out_shape=(
            jax.ShapeDtypeStruct((chips, 2, span), BF16),
            jax.ShapeDtypeStruct((tok_rows, depth), F32),
            jax.ShapeDtypeStruct((tok_rows, depth), F32),
        ),
        in_specs=[VMEM] * 4,
        out_specs=(VMEM,) * 3,
        compiler_params=params(32),
        cost_estimate=pl.CostEstimate(
            flops=6 * tok_rows * depth * width, bytes_accessed=3 * tok_rows * width, transcendentals=tok_rows * width
        ),
        name="backward",
    )(inputs, upstream, got, slab)
    parts = lax.all_to_all(term, "chip", 0, 0, tiled=True, axis_index_groups=[order])
    own, other = pl.pallas_call(
        sum_kernel,
        out_shape=(
            jax.ShapeDtypeStruct((1, span), F32),
            jax.ShapeDtypeStruct((tok_rows + 16, LANES), F32),
        ),
        in_specs=[SMEM, VMEM, VMEM],
        out_specs=(VMEM, VMEM),
        compiler_params=params(8),
        name="sum",
    )(core, parts, theirs)
    both = lax.all_gather(other, "core", axis=0, tiled=False)
    spread, kept = pl.pallas_call(
        lambda *refs: select_kernel(tok_rows, *refs),
        out_shape=(
            jax.ShapeDtypeStruct((groups, tiles, LANES), BF16),
            jax.ShapeDtypeStruct((tiles, LANES), F32),
        ),
        in_specs=[SMEM] + [VMEM] * 5,
        out_specs=(VMEM, VMEM),
        compiler_params=params(8),
        name="select",
    )(core, own, both, carried, mask, table)
    back = lax.all_to_all(spread, "rep", 0, 0, tiled=True, axis_index_groups=[middle_out])
    update, new_momentum, dacts = pl.pallas_call(
        finish_kernel,
        out_shape=(
            jax.ShapeDtypeStruct((1, width), F32),
            jax.ShapeDtypeStruct((1, width), F32),
            jax.ShapeDtypeStruct((tok_rows, depth), BF16),
        ),
        in_specs=[SMEM] + [VMEM] * 5,
        out_specs=(VMEM, VMEM, VMEM),
        compiler_params=params(8),
        name="finish",
    )(core, back, kept, mine, both, place)
    return (new_momentum[None], dacts[None], update)


def solution(mesh):
    shape = (mesh.shape["fsdp"] // 2, 2, mesh.shape["rep"])
    split = Mesh(mesh.devices.reshape(shape), (*ROWS, "rep"))
    placed = (
        P("rep", ROWS, None),
        P("rep", ROWS, None),
        P(ROWS, None),
        P("rep", ROWS, None),
        P("rep", ROWS, None, None),
    )
    return jax.shard_map(
        local,
        mesh=split,
        in_specs=placed,
        out_specs=(P("rep", ROWS, None), P("rep", ROWS, None), P(ROWS, None)),
        check_vma=False,
    )
```

```python
import math

import jax
import jax.numpy as jnp
import numpy as np
from jax import lax
from jax.experimental import pallas as pl
from jax.experimental.pallas import tpu as pltpu
from jax.sharding import Mesh
from jax.sharding import PartitionSpec as P

ROWS = ("chip", "core")
LANES = 128
HIGHEST = lax.Precision.HIGHEST
TURNED = (((1,), (1,)), ((), ()))
F32 = jnp.float32
BF16 = jnp.bfloat16
VMEM = pl.BlockSpec(memory_space=pltpu.VMEM)
SMEM = pl.BlockSpec(memory_space=pltpu.SMEM)


def params(mib):
    return pltpu.CompilerParams(vmem_limit_bytes=mib * 1024 * 1024)


def dct_table(length):
    index = np.arange(length)
    freq = index[:, None]
    factor = np.where(freq == 0, np.sqrt(1.0 / length), np.sqrt(2.0 / length))
    table = factor * np.cos(np.pi * (index[None, :] + 0.5) * freq / length)
    return np.kron(np.eye(LANES // length), table).astype(np.float32)


def half_placed(order):
    count = 2 * len(order)
    table = np.zeros((count, count), np.float32)
    for i, chip in enumerate(order):
        for c in range(2):
            table[2 * chip + c, 2 * i + c] = 0.5
    return table.astype(BF16)


def grid_of(shape):
    return [lax.broadcasted_iota(jnp.int32, shape, dim) for dim in range(2)]


def send_kernel(core_ref, pair_ref, out_ref):
    cores, span = out_ref.shape[1:]
    half = pl.ds(pl.multiple_of(core_ref[0] * span, LANES), span)
    rows = jnp.concatenate([pair_ref[c, :, half] for c in range(cores)], axis=0)
    out_ref[...] = jnp.broadcast_to(rows[None], out_ref.shape)


def unpack_kernel(slab_ref, out_ref):
    out_ref[...] = slab_ref[...].reshape(out_ref.shape)


def backward_kernel(scale, acts_ref, cotan_ref, got_ref, slab_ref, term_ref, mine_ref, theirs_ref):
    depth, span = slab_ref.shape
    slab = slab_ref[...]
    total = None
    for side, back_ref in enumerate((mine_ref, theirs_ref)):
        acts = acts_ref[...] if side == 0 else got_ref[:, span:]
        upstream = cotan_ref[...] if side == 0 else got_ref[:, :span]
        mid = jnp.dot(acts, slab, preferred_element_type=F32)
        t = jnp.tanh(mid)
        slope = (1.0 + t) * (1.0 + mid * (1.0 - t))
        dpre = (upstream.astype(F32) * slope).astype(BF16)
        back_ref[...] = lax.dot_general(dpre, slab, TURNED, preferred_element_type=F32)
        term = jnp.dot(acts.T, dpre, preferred_element_type=F32)
        total = term if total is None else total + term
    term_ref[...] = (total * scale).astype(BF16).reshape(term_ref.shape)


def sum_kernel(core_ref, parts_ref, theirs_ref, own_ref, out_ref):
    chips, rows, span = parts_ref.shape
    toks = theirs_ref.shape[0]
    row, col = grid_of((8, chips * rows))
    wanted = jnp.where(row == 0, core_ref[0], 1 - core_ref[0])
    pick = jnp.where(col % rows == wanted, 1.0, 0.0).astype(BF16)
    grad = jnp.dot(pick, parts_ref[...].reshape(chips * rows, span), preferred_element_type=F32)
    own_ref[...] = grad[:1]
    out_ref[:toks, :] = theirs_ref[...]
    tiles = span // LANES
    pad = jnp.zeros((out_ref.shape[0] - toks - tiles, LANES), F32)
    other = [grad[1:2, q * LANES : (q + 1) * LANES] for q in range(tiles)]
    out_ref[toks:, :] = jnp.concatenate([*other, pad], axis=0)


def select_kernel(toks, core_ref, own_ref, both_ref, carried_ref, mask_ref, table_ref, spread_ref, kept_ref):
    tiles = own_ref.shape[1] // LANES
    got = both_ref[1 - core_ref[0], toks:, :]
    first = core_ref[0] == 0
    tiled = []
    for q in range(tiles):
        here, there = own_ref[:, q * LANES : (q + 1) * LANES], got[q : q + 1]
        tiled += [jnp.where(first, here, there), jnp.where(first, there, here)]
    moment = carried_ref[...] + jnp.concatenate(tiled, axis=0)
    table = table_ref[...]
    coeffs = lax.dot_general(moment, table, TURNED, precision=HIGHEST, preferred_element_type=F32)
    dense = jnp.where(mask_ref[...] != 0.0, coeffs, 0.0)
    decoded = jnp.dot(dense, table, precision=HIGHEST, preferred_element_type=F32)
    spread_ref[...] = jnp.broadcast_to(decoded.astype(BF16)[None], spread_ref.shape)
    kept_ref[...] = moment - decoded


def finish_kernel(core_ref, got_ref, kept_ref, mine_ref, both_ref, place_ref, update_ref, momentum_ref, dacts_ref):
    theirs = both_ref[1 - core_ref[0], : dacts_ref.shape[0], :]
    dacts = (mine_ref[...] + theirs).astype(BF16)
    dacts_ref[...] = (lax.dot_general(dacts, place_ref[...], TURNED, preferred_element_type=F32) * 2.0).astype(BF16)
    groups, rows, lanes = got_ref.shape
    total = got_ref[0].astype(F32)
    for group in range(1, groups):
        total += got_ref[group].astype(F32)
    total = total / groups
    kept = kept_ref[...]
    for r in range(rows):
        at = (r % 2 * (rows // 2) + r // 2) * lanes
        update_ref[:, at : at + lanes] = total[r : r + 1]
        momentum_ref[:, at : at + lanes] = kept[r : r + 1]


def other_core(x):
    return lax.ppermute(x, "core", [(0, 1), (1, 0)])


def local(acts, cotan, weight, momentum, select_ids):
    tok_rows, depth = acts.shape[1:]
    width = momentum.shape[2]
    length = width // select_ids.shape[2]
    groups = lax.axis_size("rep")
    chips = lax.axis_size("chip")
    order = [chips - 1, *range(chips - 1)]
    place = half_placed(order)
    middle_out = sorted(range(groups), key=lambda g: (abs(g - groups // 2), g))
    core = lax.axis_index("core").reshape(1).astype(jnp.int32)
    scale = 1.0 / math.sqrt(lax.axis_size(ROWS) * tok_rows)
    span = width // 2
    tiles = width // LANES
    table = dct_table(length)

    pair = lax.all_gather(weight, "core", axis=0, tiled=False)
    sent = pl.pallas_call(
        send_kernel,
        out_shape=jax.ShapeDtypeStruct((chips, 2, span), BF16),
        in_specs=[SMEM, VMEM],
        out_specs=VMEM,
        compiler_params=params(8),
        name="send",
    )(core, pair)
    slab = lax.all_to_all(sent, "chip", 0, 0, tiled=True, axis_index_groups=[order])
    carried = (0.9 * momentum).reshape(2, tiles // 2, LANES).transpose(1, 0, 2).reshape(tiles, LANES)
    ids = select_ids.reshape(2, tiles // 2, LANES // length, -1).transpose(1, 0, 2, 3)
    mask = jnp.any(ids[..., None] == jnp.arange(length), axis=3)
    mask = mask.reshape(tiles, LANES).astype(F32)
    half = jnp.asarray(0.5, BF16)
    first = core[0] == 0
    low, high = cotan[0][:, :span] * half, cotan[0][:, span:] * half
    inputs = jnp.dot(acts[0], place, preferred_element_type=F32).astype(BF16)
    got = other_core(jnp.concatenate([jnp.where(first, high, low), inputs], axis=1))
    slab, carried, mask, upstream, inputs = lax.optimization_barrier(
        (slab, carried, mask, jnp.where(first, low, high), inputs)
    )
    slab = pl.pallas_call(
        unpack_kernel,
        out_shape=jax.ShapeDtypeStruct((depth, span), BF16),
        in_specs=[VMEM],
        out_specs=VMEM,
        compiler_params=params(8),
        cost_estimate=pl.CostEstimate(flops=1 << 36, bytes_accessed=0, transcendentals=0),
        name="unpack",
    )(slab)
    term, mine, theirs = pl.pallas_call(
        lambda *refs: backward_kernel(scale * 2.0, *refs),
        out_shape=(
            jax.ShapeDtypeStruct((chips, 2, span), BF16),
            jax.ShapeDtypeStruct((tok_rows, depth), F32),
            jax.ShapeDtypeStruct((tok_rows, depth), F32),
        ),
        in_specs=[VMEM] * 4,
        out_specs=(VMEM,) * 3,
        compiler_params=params(32),
        cost_estimate=pl.CostEstimate(
            flops=6 * tok_rows * depth * width, bytes_accessed=3 * tok_rows * width, transcendentals=tok_rows * width
        ),
        name="backward",
    )(inputs, upstream, got, slab)
    parts = lax.all_to_all(term, "chip", 0, 0, tiled=True, axis_index_groups=[order])
    own, other = pl.pallas_call(
        sum_kernel,
        out_shape=(
            jax.ShapeDtypeStruct((1, span), F32),
            jax.ShapeDtypeStruct((tok_rows + 16, LANES), F32),
        ),
        in_specs=[SMEM, VMEM, VMEM],
        out_specs=(VMEM, VMEM),
        compiler_params=params(8),
        name="sum",
    )(core, parts, theirs)
    both = lax.all_gather(other, "core", axis=0, tiled=False)
    spread, kept = pl.pallas_call(
        lambda *refs: select_kernel(tok_rows, *refs),
        out_shape=(
            jax.ShapeDtypeStruct((groups, tiles, LANES), BF16),
            jax.ShapeDtypeStruct((tiles, LANES), F32),
        ),
        in_specs=[SMEM] + [VMEM] * 5,
        out_specs=(VMEM, VMEM),
        compiler_params=params(8),
        name="select",
    )(core, own, both, carried, mask, table)
    back = lax.all_to_all(spread, "rep", 0, 0, tiled=True, axis_index_groups=[middle_out])
    update, new_momentum, dacts = pl.pallas_call(
        finish_kernel,
        out_shape=(
            jax.ShapeDtypeStruct((1, width), F32),
            jax.ShapeDtypeStruct((1, width), F32),
            jax.ShapeDtypeStruct((tok_rows, depth), BF16),
        ),
        in_specs=[SMEM] + [VMEM] * 5,
        out_specs=(VMEM, VMEM, VMEM),
        compiler_params=params(8),
        name="finish",
    )(core, back, kept, mine, both, place)
    return (new_momentum[None], dacts[None], update)


def solution(mesh):
    shape = (mesh.shape["fsdp"] // 2, 2, mesh.shape["rep"])
    split = Mesh(mesh.devices.reshape(shape), (*ROWS, "rep"))
    placed = (
        P("rep", ROWS, None),
        P("rep", ROWS, None),
        P(ROWS, None),
        P("rep", ROWS, None),
        P("rep", ROWS, None, None),
    )
    return jax.shard_map(
        local,
        mesh=split,
        in_specs=placed,
        out_specs=(P("rep", ROWS, None), P("rep", ROWS, None), P(ROWS, None)),
        check_vma=False,
    )
```
